512 devices in a mesh: rep: 64 (over z, x_lo, core), fsdp: 8 (over x_hi, y).
Axes of the slice: x: 4 (x_hi: 2, x_lo: 2; x = x_hi * 2 + x_lo), y: 4, z: 16, core: 2. Of those that a mesh axis runs over, the one named last changes fastest.
Arguments:
- step: int32 [1], replicated, may hold values from 0 to 999
- numerator: float32 [64, 512, 1024], P('rep', 'fsdp'), may hold values from -6 to 6
- weight: float32 [64], P('rep'), may hold values from 0.25 to 4
- moment1: float32 [64, 512, 1024], P('rep', 'fsdp'), may hold values from -4 to 4
- moment2: float32 [64, 512, 1024], P('rep', 'fsdp'), may hold values from 0.01 to 1
- grads: bfloat16 [64, 8, 512, 1024], P('rep', 'fsdp'), may hold values from -6 to 6
Outputs:
- new_numerator: float32 [64, 512, 1024], P('rep', 'fsdp')
- new_weight: float32 [64], P('rep')
- debiased: bfloat16 [64, 512, 1024], P('rep', 'fsdp')
- new_moment1: float32 [64, 512, 1024], P('rep', 'fsdp')
- new_moment2: float32 [64, 512, 1024], P('rep', 'fsdp')
The draws below stay inside these ranges and needn't reach their ends.
Inputs may be any that keep to these rules, and one draw needn't show every extreme that they name: t is a step index.
All inputs are finite; a program needn't handle non-finite values.
Results may differ from the reference program's by a relative error of at most 0.013.
Values may be sent and summed in bfloat16 or wider, within the bound.
No kernel may reach another device: no remote copies, remote signals or barrier semaphores. Data moves between devices by JAX's collectives and lax.ppermute only.
A program may use at most 64 MiB of HBM per device.

```python
import math
import jax
import jax.numpy as jnp
from jax import lax

LANES = 1024
ROWS = 512
REPLICAS = 64
N_REP = 64
N_FSDP = 8


def spiked(values, rng, source, target, shards_of, factor):
    owner, partner = [(jnp.arange(values.shape[dim]) // (values.shape[dim] // shards_of)).reshape([-1 if axis == dim else 1 for axis in range(values.ndim)]) for dim in (source, target)]
    chosen = jax.random.permutation(rng, shards_of)[partner]
    strong = (owner == chosen) | (owner == (partner + shards_of // 2) % shards_of)
    return jnp.where(strong, factor * values, values)


def steps_of(own_key, shape, cuts, low, high):
    level = 1.0
    for dim, parts in cuts:
        heights = jax.random.uniform(jax.random.fold_in(jax.random.fold_in(own_key, 6), dim), (parts,), jnp.float32, low / len(cuts), high / len(cuts))
        level = level * jnp.repeat(jnp.exp(heights), shape[dim] // parts).reshape((-1,) + (1,) * (len(shape) - 1 - dim))
    return level


def bell_draw(stream_key, extent, width, reach, shards=(), held_as=jnp.bfloat16):
    values = jax.random.normal(stream_key, extent, jnp.float32) * width
    if len(shards) > 0:
        values = steps_of(stream_key, extent, shards, -0.22, 0.18) * values
    return jnp.clip(values, min=-reach, max=reach).astype(held_as)


def bell_draw_with(own_key, shape, deviation, most, split, heavy, kind=jnp.bfloat16):
    values = deviation * jax.random.normal(own_key, shape, jnp.float32)
    if split:
        values = values * steps_of(own_key, shape, split, -0.22, 0.18)
    return jnp.clip(spiked(values, jax.random.fold_in(own_key, 3), *heavy), -most, most).astype(kind)


def setup_inputs(seed: int = 0) -> dict:
    key_of = jax.random.split(jax.random.key(seed), 7)
    return {
        "step": jax.random.randint(key_of[0], (1,), 0, 1000).astype(jnp.int32),
        "numerator": bell_draw(key_of[1], (REPLICAS, ROWS, LANES), 1.0, 6.0, ((0, 64), (1, 8)), jnp.float32),
        "weight": jnp.clip(jnp.exp(math.log(4.0) - 2.7725887 * jax.random.uniform(key_of[2], (REPLICAS,), jnp.float32) ** steps_of(key_of[2], (REPLICAS,), ((0, 64),), -0.2, 0.2)), 0.25, 4.0),
        "moment1": bell_draw(key_of[3], (REPLICAS, ROWS, LANES), 0.3, 4.0, ((0, 64), (1, 8)), jnp.float32),
        "moment2": jnp.clip(jnp.exp(math.log(1.0) - 4.6051702 * jax.random.uniform(key_of[4], (REPLICAS, ROWS, LANES), jnp.float32) ** steps_of(key_of[4], (REPLICAS, ROWS, LANES), ((0, 64), (1, 8)), -0.2, 0.2)), 0.01, 1.0),
        "grads": bell_draw_with(key_of[5], (REPLICAS, N_FSDP, ROWS, LANES), 1.0, 6.0, ((0, 64), (1, 8)), (1, 2, 8, 2.0)),
    }


def reference(step, numerator, weight, moment1, moment2, grads):
    gradient = lax.optimization_barrier(jnp.sum(grads, axis=1, dtype=jnp.float32)) / N_FSDP
    new_moment1 = 0.9 * moment1 + 0.1 * gradient
    new_moment2 = 0.95 * moment2 + 0.05 * gradient * gradient
    count = (step[0] + 1).astype(jnp.float32)
    first_corr = 1.0 - jnp.power(jnp.float32(0.9), count)
    second_corr = 1.0 - jnp.power(jnp.float32(0.95), count)
    update = 0.05 * (new_moment1 / first_corr / (jnp.sqrt(new_moment2 / second_corr) + 1e-08) + 0.1 * numerator)
    half = numerator - update
    levels = N_REP.bit_length() - 1
    offset = jnp.left_shift(jnp.int32(1), (step[0] % levels).astype(jnp.int32))
    new_numerator = 0.5 * (half + jnp.roll(half, offset, axis=0))
    new_weight = 0.5 * (weight + jnp.roll(weight, offset, axis=0))
    debiased = (new_numerator / new_weight[:, None, None]).astype(jnp.bfloat16)
    return (new_numerator, new_weight, debiased, new_moment1, new_moment2)
```

```python
from functools import partial

import jax
import jax.numpy as jnp
from jax import lax
from jax.sharding import PartitionSpec as P


def shifted(value, axis, steps):
    count = lax.axis_size(axis)
    pairs = [(source, (source + steps) % count) for source in range(count)]
    return lax.ppermute(value, axis, pairs)


def split_in_pieces(weight):
    high = weight.astype(jnp.bfloat16)
    rest = weight - high.astype(jnp.float32)
    middle = rest.astype(jnp.bfloat16)
    low = (rest - middle.astype(jnp.float32)).astype(jnp.bfloat16)
    return high, middle, low


def mix_after(half, weight, offset):
    sent = shifted(half.astype(jnp.bfloat16), "rep", offset)
    sent_weight = shifted(weight, "rep", offset)
    return sent, sent_weight


def local(step, numerator, weight, moment1, moment2, grads):
    levels = lax.axis_size("rep").bit_length() - 1
    n_fsdp = lax.axis_size("fsdp")
    phase = step[0] % levels
    rows = numerator.shape[1]
    blocks = grads.reshape(n_fsdp, rows, -1)
    landed = lax.all_to_all(blocks, "fsdp", split_axis=0, concat_axis=0, tiled=True)
    gradient = jnp.sum(landed, axis=0, dtype=jnp.float32)[None] / n_fsdp
    new_moment1 = 0.9 * moment1 + 0.1 * gradient
    new_moment2 = 0.95 * moment2 + 0.05 * gradient * gradient
    count = (step[0] + 1).astype(jnp.float32)
    first_corr = 1.0 - jnp.power(jnp.float32(0.9), count)
    second_corr = 1.0 - jnp.power(jnp.float32(0.95), count)
    update = 0.05 * (
        new_moment1 / first_corr / (jnp.sqrt(new_moment2 / second_corr) + 1e-08) + 0.1 * numerator
    )
    half = numerator - update
    after_branches = [partial(mix_after, offset=1 << level) for level in range(levels)]
    half_partner, weight_partner = lax.switch(phase, after_branches, half, weight)
    new_numerator = 0.5 * (half + half_partner.astype(jnp.float32))
    new_weight = 0.5 * (weight + weight_partner)
    debiased = (new_numerator / new_weight[:, None, None]).astype(jnp.bfloat16)
    return (new_numerator, new_weight, debiased, new_moment1, new_moment2)


def solution(mesh):
    in_specs = (
        P(),
        P("rep", "fsdp", None),
        P("rep"),
        P("rep", "fsdp", None),
        P("rep", "fsdp", None),
        P("rep", "fsdp", None, None),
    )
    out_specs = (
        P("rep", "fsdp", None),
        P("rep"),
        P("rep", "fsdp", None),
        P("rep", "fsdp", None),
        P("rep", "fsdp", None),
    )
    return jax.shard_map(local, mesh=mesh, in_specs=in_specs, out_specs=out_specs, check_vma=False)
```

```python
from functools import partial

import jax
import jax.numpy as jnp
from jax import lax
from jax.experimental import pallas as pl
from jax.experimental.pallas import tpu as pltpu
from jax.sharding import PartitionSpec as P

TILE_ROWS = 16
TILE_LANES = 128


def shifted(value, axis, steps):
    count = lax.axis_size(axis)
    pairs = [(source, (source + steps) % count) for source in range(count)]
    return lax.ppermute(value, axis, pairs)


def tiles_of(shape):
    across = shape[1] // TILE_LANES
    for down in range(shape[0] // TILE_ROWS):
        for column in range(across):
            rows = pl.ds(down * TILE_ROWS, TILE_ROWS)
            lanes = pl.ds(column * TILE_LANES, TILE_LANES)
            packed = pl.ds((down * across + column) * TILE_ROWS, TILE_ROWS)
            yield rows, lanes, packed


def moments_of(landed_ref, moment1_ref, moment2_ref, rows, lanes):
    sources = landed_ref.shape[0]
    total = landed_ref[0, rows, lanes].astype(jnp.float32)
    for source in range(1, sources):
        total = total + landed_ref[source, rows, lanes].astype(jnp.float32)
    gradient = total * (1.0 / sources)
    new_moment1 = 0.9 * moment1_ref[rows, lanes] + 0.1 * gradient
    new_moment2 = 0.95 * moment2_ref[rows, lanes] + 0.05 * gradient * gradient
    return new_moment1, new_moment2


def moments_kernel(landed_ref, moment1_ref, moment2_ref, new_moment1_ref, new_moment2_ref):
    for rows, lanes, _ in tiles_of(moment1_ref.shape):
        new_moment1, new_moment2 = moments_of(landed_ref, moment1_ref, moment2_ref, rows, lanes)
        new_moment1_ref[rows, lanes] = new_moment1
        new_moment2_ref[rows, lanes] = new_moment2


def adam_kernel(
    corr1_ref, corr2_ref, weight_ref, landed_ref, numerator_ref, moment1_ref, moment2_ref,
    half_ref, payload_ref,
):
    scale1 = 1.0 / jnp.full((1, TILE_LANES), corr1_ref[0], jnp.float32)
    scale2 = 1.0 / jnp.full((1, TILE_LANES), corr2_ref[0], jnp.float32)
    for rows, lanes, packed in tiles_of(numerator_ref.shape):
        new_moment1, new_moment2 = moments_of(landed_ref, moment1_ref, moment2_ref, rows, lanes)
        numerator = numerator_ref[rows, lanes]
        step = new_moment1 * scale1 / (jnp.sqrt(new_moment2 * scale2) + 1e-08)
        half = numerator - 0.05 * (step + 0.1 * numerator)
        half_ref[rows, lanes] = half
        payload_ref[packed, :] = half.astype(jnp.bfloat16)
    whole = jnp.full((TILE_ROWS, TILE_LANES), weight_ref[0], jnp.float32)
    high = whole.astype(jnp.bfloat16).astype(jnp.float32)
    middle = (whole - high).astype(jnp.bfloat16).astype(jnp.float32)
    low = whole - high - middle
    row = lax.broadcasted_iota(jnp.int32, whole.shape, 0)
    terms = jnp.where(row == 0, high, jnp.where(row == 1, middle, low))
    payload_ref[pl.ds(payload_ref.shape[0] - TILE_ROWS, TILE_ROWS), :] = terms.astype(jnp.bfloat16)


def mix_kernel(weight_ref, half_ref, partner_ref, new_numerator_ref, new_weight_ref, debiased_ref):
    tail = pl.ds(partner_ref.shape[0] - TILE_ROWS, TILE_ROWS)
    terms = partner_ref[tail, :].astype(jnp.float32)
    partner_weight = terms[0:1] + (terms[1:2] + terms[2:3])
    new_weight = 0.5 * (jnp.full_like(partner_weight, weight_ref[0]) + partner_weight)
    new_weight_ref[0] = new_weight[0, 0]
    scale = 1.0 / new_weight
    for rows, lanes, packed in tiles_of(half_ref.shape):
        mixed = 0.5 * (half_ref[rows, lanes] + partner_ref[packed, :].astype(jnp.float32))
        new_numerator_ref[rows, lanes] = mixed
        debiased_ref[rows, lanes] = (mixed * scale).astype(jnp.bfloat16)


def spec(space):
    return pl.BlockSpec(memory_space=space)


def call(kernel, out_shape, in_specs, out_specs, cost):
    return pl.pallas_call(
        kernel,
        out_shape=out_shape,
        in_specs=in_specs,
        out_specs=out_specs,
        compiler_params=pltpu.CompilerParams(vmem_limit_bytes=8 << 20),
        cost_estimate=pl.CostEstimate(flops=cost, bytes_accessed=cost, transcendentals=0),
        name=kernel.__name__,
    )


def exchanged(weight, landed, moment1, moment2, half, payload, offset):
    shard = jax.ShapeDtypeStruct(half.shape, jnp.float32)
    scalars, arrays = spec(pltpu.SMEM), spec(pltpu.VMEM)
    partner = shifted(payload, "rep", offset)
    new_moment1, new_moment2 = call(
        moments_kernel, (shard, shard), [arrays] * 3, (arrays,) * 2, 4 * landed.size
    )(landed, moment1, moment2)
    new_numerator, new_weight, debiased = call(
        mix_kernel,
        (shard, jax.ShapeDtypeStruct((1,), jnp.float32), jax.ShapeDtypeStruct(half.shape, jnp.bfloat16)),
        [scalars] + [arrays] * 2,
        (arrays, scalars, arrays),
        8 * half.size,
    )(weight, half, partner)
    return (new_numerator[None], new_weight, debiased[None], new_moment1[None], new_moment2[None])


def local(step, numerator, weight, moment1, moment2, grads):
    levels = lax.axis_size("rep").bit_length() - 1
    n_fsdp = lax.axis_size("fsdp")
    rows, columns = numerator.shape[1:]
    count = (step + 1).astype(jnp.float32)
    first_corr = 1.0 - jnp.power(jnp.float32(0.9), count)
    second_corr = 1.0 - jnp.power(jnp.float32(0.95), count)
    blocks = grads.reshape(n_fsdp, rows, columns)
    landed = lax.all_to_all(blocks, "fsdp", split_axis=0, concat_axis=0, tiled=True)
    shard = jax.ShapeDtypeStruct((rows, columns), jnp.float32)
    packed_rows = rows * columns // TILE_LANES + TILE_ROWS
    scalars, arrays = spec(pltpu.SMEM), spec(pltpu.VMEM)
    half, payload = call(
        adam_kernel,
        (shard, jax.ShapeDtypeStruct((packed_rows, TILE_LANES), jnp.bfloat16)),
        [scalars] * 3 + [arrays] * 4,
        (arrays,) * 2,
        4 * landed.size,
    )(first_corr, second_corr, weight, landed, numerator[0], moment1[0], moment2[0])
    branches = [partial(exchanged, offset=1 << level) for level in range(levels)]
    return lax.switch(
        step[0] % levels, branches, weight, landed, moment1[0], moment2[0], half, payload
    )


def solution(mesh):
    in_specs = (
        P(),
        P("rep", "fsdp", None),
        P("rep"),
        P("rep", "fsdp", None),
        P("rep", "fsdp", None),
        P("rep", "fsdp", None, None),
    )
    out_specs = (
        P("rep", "fsdp", None),
        P("rep"),
        P("rep", "fsdp", None),
        P("rep", "fsdp", None),
        P("rep", "fsdp", None),
    )
    return jax.shard_map(local, mesh=mesh, in_specs=in_specs, out_specs=out_specs, check_vma=False)
```

```python
from functools import partial

import jax
import jax.numpy as jnp
from jax import lax
from jax.experimental import pallas as pl
from jax.experimental.pallas import tpu as pltpu
from jax.sharding import PartitionSpec as P

TILE_ROWS = 16
TILE_LANES = 128


def shifted(value, axis, steps):
    count = lax.axis_size(axis)
    pairs = [(source, (source + steps) % count) for source in range(count)]
    return lax.ppermute(value, axis, pairs)


def tiles_of(shape):
    across = shape[1] // TILE_LANES
    for down in range(shape[0] // TILE_ROWS):
        for column in range(across):
            rows = pl.ds(down * TILE_ROWS, TILE_ROWS)
            lanes = pl.ds(column * TILE_LANES, TILE_LANES)
            packed = pl.ds((down * across + column) * TILE_ROWS, TILE_ROWS)
            yield rows, lanes, packed


def moments_of(landed_ref, moment1_ref, moment2_ref, rows, lanes):
    sources = landed_ref.shape[0]
    total = landed_ref[0, rows, lanes].astype(jnp.float32)
    for source in range(1, sources):
        total = total + landed_ref[source, rows, lanes].astype(jnp.float32)
    gradient = total * (1.0 / sources)
    new_moment1 = 0.9 * moment1_ref[rows, lanes] + 0.1 * gradient
    new_moment2 = 0.95 * moment2_ref[rows, lanes] + 0.05 * gradient * gradient
    return new_moment1, new_moment2


def moments_kernel(landed_ref, moment1_ref, moment2_ref, new_moment1_ref, new_moment2_ref):
    for rows, lanes, _ in tiles_of(moment1_ref.shape):
        new_moment1, new_moment2 = moments_of(landed_ref, moment1_ref, moment2_ref, rows, lanes)
        new_moment1_ref[rows, lanes] = new_moment1
        new_moment2_ref[rows, lanes] = new_moment2


def adam_kernel(
    corr1_ref, corr2_ref, weight_ref, landed_ref, numerator_ref, moment1_ref, moment2_ref,
    half_ref, payload_ref,
):
    scale1 = 1.0 / jnp.full((1, TILE_LANES), corr1_ref[0], jnp.float32)
    scale2 = 1.0 / jnp.full((1, TILE_LANES), corr2_ref[0], jnp.float32)
    for rows, lanes, packed in tiles_of(numerator_ref.shape):
        new_moment1, new_moment2 = moments_of(landed_ref, moment1_ref, moment2_ref, rows, lanes)
        numerator = numerator_ref[rows, lanes]
        step = new_moment1 * scale1 / (jnp.sqrt(new_moment2 * scale2) + 1e-08)
        half = numerator - 0.05 * (step + 0.1 * numerator)
        half_ref[rows, lanes] = half
        payload_ref[packed, :] = half.astype(jnp.bfloat16)
    whole = jnp.full((TILE_ROWS, TILE_LANES), weight_ref[0], jnp.float32)
    high = whole.astype(jnp.bfloat16).astype(jnp.float32)
    middle = (whole - high).astype(jnp.bfloat16).astype(jnp.float32)
    low = whole - high - middle
    row = lax.broadcasted_iota(jnp.int32, whole.shape, 0)
    terms = jnp.where(row == 0, high, jnp.where(row == 1, middle, low))
    payload_ref[pl.ds(payload_ref.shape[0] - TILE_ROWS, TILE_ROWS), :] = terms.astype(jnp.bfloat16)


def weight_in(payload_ref):
    tail = pl.ds(payload_ref.shape[0] - TILE_ROWS, TILE_ROWS)
    terms = payload_ref[tail, :].astype(jnp.float32)
    return terms[0:1] + (terms[1:2] + terms[2:3])


def mix_kernel(half_ref, own_ref, partner_ref, new_numerator_ref, new_weight_ref, debiased_ref):
    new_weight = 0.5 * (weight_in(own_ref) + weight_in(partner_ref))
    new_weight_ref[0] = new_weight[0, 0]
    scale = 1.0 / new_weight
    for rows, lanes, packed in tiles_of(half_ref.shape):
        mixed = 0.5 * (half_ref[rows, lanes] + partner_ref[packed, :].astype(jnp.float32))
        new_numerator_ref[rows, lanes] = mixed
        debiased_ref[rows, lanes] = (mixed * scale).astype(jnp.bfloat16)


def spec(space):
    return pl.BlockSpec(memory_space=space)


def call(kernel, out_shape, in_specs, out_specs, cost):
    return pl.pallas_call(
        kernel,
        out_shape=out_shape,
        in_specs=in_specs,
        out_specs=out_specs,
        compiler_params=pltpu.CompilerParams(vmem_limit_bytes=8 << 20),
        cost_estimate=pl.CostEstimate(flops=cost, bytes_accessed=cost, transcendentals=0),
        name=kernel.__name__,
    )


def exchanged(landed, moment1, moment2, half, payload, offset):
    shard = jax.ShapeDtypeStruct(half.shape, jnp.float32)
    scalars, arrays = spec(pltpu.SMEM), spec(pltpu.VMEM)
    partner = shifted(payload, "rep", offset)
    new_moment1, new_moment2 = call(
        moments_kernel, (shard, shard), [arrays] * 3, (arrays,) * 2, 4 * landed.size
    )(landed, moment1, moment2)
    new_numerator, new_weight, debiased = call(
        mix_kernel,
        (shard, jax.ShapeDtypeStruct((1,), jnp.float32), jax.ShapeDtypeStruct(half.shape, jnp.bfloat16)),
        [arrays] * 3,
        (arrays, scalars, arrays),
        8 * half.size,
    )(half, payload, partner)
    return (new_numerator[None], new_weight, debiased[None], new_moment1[None], new_moment2[None])


def local(step, numerator, weight, moment1, moment2, grads):
    levels = lax.axis_size("rep").bit_length() - 1
    n_fsdp = lax.axis_size("fsdp")
    rows, columns = numerator.shape[1:]
    count = (step + 1).astype(jnp.float32)
    first_corr = 1.0 - jnp.power(jnp.float32(0.9), count)
    second_corr = 1.0 - jnp.power(jnp.float32(0.95), count)
    blocks = grads.reshape(n_fsdp, rows, columns)
    landed = lax.all_to_all(blocks, "fsdp", split_axis=0, concat_axis=0, tiled=True)
    shard = jax.ShapeDtypeStruct((rows, columns), jnp.float32)
    packed_rows = rows * columns // TILE_LANES + TILE_ROWS
    scalars, arrays = spec(pltpu.SMEM), spec(pltpu.VMEM)
    half, payload = call(
        adam_kernel,
        (shard, jax.ShapeDtypeStruct((packed_rows, TILE_LANES), jnp.bfloat16)),
        [scalars] * 3 + [arrays] * 4,
        (arrays,) * 2,
        4 * landed.size,
    )(first_corr, second_corr, weight, landed, numerator[0], moment1[0], moment2[0])
    branches = [partial(exchanged, offset=1 << level) for level in range(levels)]
    return lax.switch(
        step[0] % levels, branches, landed, moment1[0], moment2[0], half, payload
    )


def solution(mesh):
    in_specs = (
        P(),
        P("rep", "fsdp", None),
        P("rep"),
        P("rep", "fsdp", None),
        P("rep", "fsdp", None),
        P("rep", "fsdp", None, None),
    )
    out_specs = (
        P("rep", "fsdp", None),
        P("rep"),
        P("rep", "fsdp", None),
        P("rep", "fsdp", None),
        P("rep", "fsdp", None),
    )
    return jax.shard_map(local, mesh=mesh, in_specs=in_specs, out_specs=out_specs, check_vma=False)
```

```python
from functools import partial

import jax
import jax.numpy as jnp
from jax import lax
from jax.experimental import pallas as pl
from jax.experimental.pallas import tpu as pltpu
from jax.sharding import PartitionSpec as P

TILE_ROWS = 16
TILE_LANES = 128


def shifted(value, axis, steps):
    count = lax.axis_size(axis)
    around = [(source, source + steps - count) for source in range(count - steps, count)]
    onward = [(source, source + steps) for source in range(count - steps)]
    if 2 * steps == count:
        return (lax.ppermute(value, axis, around + onward),)
    return lax.ppermute(value, axis, onward), lax.ppermute(value, axis, around)


def tiles_of(shape):
    across = shape[1] // TILE_LANES
    for down in range(shape[0] // TILE_ROWS):
        for column in range(across):
            rows = pl.ds(down * TILE_ROWS, TILE_ROWS)
            lanes = pl.ds(column * TILE_LANES, TILE_LANES)
            packed = pl.ds((down * across + column) * TILE_ROWS, TILE_ROWS)
            yield rows, lanes, packed


def moments_of(landed_ref, moment1_ref, moment2_ref, rows, lanes):
    sources = landed_ref.shape[0]
    total = landed_ref[0, rows, lanes].astype(jnp.float32)
    for source in range(1, sources):
        total = total + landed_ref[source, rows, lanes].astype(jnp.float32)
    gradient = total * (1.0 / sources)
    new_moment1 = 0.9 * moment1_ref[rows, lanes] + 0.1 * gradient
    new_moment2 = 0.95 * moment2_ref[rows, lanes] + 0.05 * gradient * gradient
    return new_moment1, new_moment2


def moments_kernel(landed_ref, moment1_ref, moment2_ref, new_moment1_ref, new_moment2_ref):
    for rows, lanes, _ in tiles_of(moment1_ref.shape):
        new_moment1, new_moment2 = moments_of(landed_ref, moment1_ref, moment2_ref, rows, lanes)
        new_moment1_ref[rows, lanes] = new_moment1
        new_moment2_ref[rows, lanes] = new_moment2


def adam_kernel(
    corr1_ref, corr2_ref, weight_ref, landed_ref, numerator_ref, moment1_ref, moment2_ref,
    half_ref, payload_ref,
):
    scale1 = 1.0 / jnp.full((1, TILE_LANES), corr1_ref[0], jnp.float32)
    scale2 = 1.0 / jnp.full((1, TILE_LANES), corr2_ref[0], jnp.float32)
    for rows, lanes, packed in tiles_of(numerator_ref.shape):
        new_moment1, new_moment2 = moments_of(landed_ref, moment1_ref, moment2_ref, rows, lanes)
        numerator = numerator_ref[rows, lanes]
        step = new_moment1 * scale1 / (jnp.sqrt(new_moment2 * scale2) + 1e-08)
        half = numerator - 0.05 * (step + 0.1 * numerator)
        half_ref[rows, lanes] = half
        payload_ref[packed, :] = half.astype(jnp.bfloat16)
    whole = jnp.full((TILE_ROWS, TILE_LANES), weight_ref[0], jnp.float32)
    high = whole.astype(jnp.bfloat16).astype(jnp.float32)
    middle = (whole - high).astype(jnp.bfloat16).astype(jnp.float32)
    low = whole - high - middle
    row = lax.broadcasted_iota(jnp.int32, whole.shape, 0)
    terms = jnp.where(row == 0, high, jnp.where(row == 1, middle, low))
    payload_ref[pl.ds(payload_ref.shape[0] - TILE_ROWS, TILE_ROWS), :] = terms.astype(jnp.bfloat16)


def received(rows, *refs):
    return sum(ref[rows, :].astype(jnp.float32) for ref in refs)


def weight_in(*refs):
    terms = received(pl.ds(refs[0].shape[0] - TILE_ROWS, TILE_ROWS), *refs)
    return terms[0:1] + (terms[1:2] + terms[2:3])


def mix_kernel(half_ref, own_ref, *refs):
    sent_refs, (new_numerator_ref, new_weight_ref, debiased_ref) = refs[:-3], refs[-3:]
    new_weight = 0.5 * (weight_in(own_ref) + weight_in(*sent_refs))
    new_weight_ref[0] = new_weight[0, 0]
    scale = 1.0 / new_weight
    for rows, lanes, packed in tiles_of(half_ref.shape):
        mixed = 0.5 * (half_ref[rows, lanes] + received(packed, *sent_refs))
        new_numerator_ref[rows, lanes] = mixed
        debiased_ref[rows, lanes] = (mixed * scale).astype(jnp.bfloat16)


def spec(space):
    return pl.BlockSpec(memory_space=space)


def call(kernel, out_shape, in_specs, out_specs, cost):
    return pl.pallas_call(
        kernel,
        out_shape=out_shape,
        in_specs=in_specs,
        out_specs=out_specs,
        compiler_params=pltpu.CompilerParams(vmem_limit_bytes=8 << 20),
        cost_estimate=pl.CostEstimate(flops=cost, bytes_accessed=cost, transcendentals=0),
        name=kernel.__name__,
    )


def exchanged(landed, moment1, moment2, half, payload, offset):
    shard = jax.ShapeDtypeStruct(half.shape, jnp.float32)
    scalars, arrays = spec(pltpu.SMEM), spec(pltpu.VMEM)
    sent = shifted(payload, "rep", offset)
    new_moment1, new_moment2 = call(
        moments_kernel, (shard, shard), [arrays] * 3, (arrays,) * 2, 4 * landed.size
    )(landed, moment1, moment2)
    new_numerator, new_weight, debiased = call(
        mix_kernel,
        (shard, jax.ShapeDtypeStruct((1,), jnp.float32), jax.ShapeDtypeStruct(half.shape, jnp.bfloat16)),
        [arrays] * (2 + len(sent)),
        (arrays, scalars, arrays),
        8 * half.size,
    )(half, payload, *sent)
    return (new_numerator[None], new_weight, debiased[None], new_moment1[None], new_moment2[None])


def local(step, numerator, weight, moment1, moment2, grads):
    levels = lax.axis_size("rep").bit_length() - 1
    n_fsdp = lax.axis_size("fsdp")
    rows, columns = numerator.shape[1:]
    count = (step + 1).astype(jnp.float32)
    first_corr = 1.0 - jnp.power(jnp.float32(0.9), count)
    second_corr = 1.0 - jnp.power(jnp.float32(0.95), count)
    blocks = grads.reshape(n_fsdp, rows, columns)
    landed = lax.all_to_all(blocks, "fsdp", split_axis=0, concat_axis=0, tiled=True)
    shard = jax.ShapeDtypeStruct((rows, columns), jnp.float32)
    packed_rows = rows * columns // TILE_LANES + TILE_ROWS
    scalars, arrays = spec(pltpu.SMEM), spec(pltpu.VMEM)
    half, payload = call(
        adam_kernel,
        (shard, jax.ShapeDtypeStruct((packed_rows, TILE_LANES), jnp.bfloat16)),
        [scalars] * 3 + [arrays] * 4,
        (arrays,) * 2,
        4 * landed.size,
    )(first_corr, second_corr, weight, landed, numerator[0], moment1[0], moment2[0])
    branches = [partial(exchanged, offset=1 << level) for level in range(levels)]
    return lax.switch(
        step[0] % levels, branches, landed, moment1[0], moment2[0], half, payload
    )


def solution(mesh):
    in_specs = (
        P(),
        P("rep", "fsdp", None),
        P("rep"),
        P("rep", "fsdp", None),
        P("rep", "fsdp", None),
        P("rep", "fsdp", None, None),
    )
    out_specs = (
        P("rep", "fsdp", None),
        P("rep"),
        P("rep", "fsdp", None),
        P("rep", "fsdp", None),
        P("rep", "fsdp", None),
    )
    return jax.shard_map(local, mesh=mesh, in_specs=in_specs, out_specs=out_specs, check_vma=False)
```

```python
from functools import partial

import jax
import jax.numpy as jnp
from jax import lax
from jax.experimental import pallas as pl
from jax.experimental.pallas import tpu as pltpu
from jax.sharding import PartitionSpec as P

TILE_ROWS = 16
TILE_LANES = 128


def shifted(value, axis, steps):
    count = lax.axis_size(axis)
    around = [(source, source + steps - count) for source in range(count - steps, count)]
    onward = [(source, source + steps) for source in range(count - steps)]
    first, second = around, onward
    if 2 * steps == count:
        first = [pair for pair in around + onward if pair[0] % 2 == 1]
        second = [pair for pair in around + onward if pair[0] % 2 == 0]
    return lax.ppermute(value, axis, second), lax.ppermute(value, axis, first)


def tiles_of(shape):
    across = shape[1] // TILE_LANES
    for down in range(shape[0] // TILE_ROWS):
        for column in range(across):
            rows = pl.ds(down * TILE_ROWS, TILE_ROWS)
            lanes = pl.ds(column * TILE_LANES, TILE_LANES)
            packed = pl.ds((down * across + column) * TILE_ROWS, TILE_ROWS)
            yield rows, lanes, packed


def moments_of(landed_ref, moment1_ref, moment2_ref, rows, lanes):
    sources = landed_ref.shape[0]
    total = landed_ref[0, rows, lanes].astype(jnp.float32)
    for source in range(1, sources):
        total = total + landed_ref[source, rows, lanes].astype(jnp.float32)
    gradient = total * (1.0 / sources)
    new_moment1 = 0.9 * moment1_ref[rows, lanes] + 0.1 * gradient
    new_moment2 = 0.95 * moment2_ref[rows, lanes] + 0.05 * gradient * gradient
    return new_moment1, new_moment2


def moments_kernel(landed_ref, moment1_ref, moment2_ref, new_moment1_ref, new_moment2_ref):
    for rows, lanes, _ in tiles_of(moment1_ref.shape):
        new_moment1, new_moment2 = moments_of(landed_ref, moment1_ref, moment2_ref, rows, lanes)
        new_moment1_ref[rows, lanes] = new_moment1
        new_moment2_ref[rows, lanes] = new_moment2


def adam_kernel(
    corr1_ref, corr2_ref, weight_ref, landed_ref, numerator_ref, moment1_ref, moment2_ref,
    half_ref, payload_ref,
):
    scale1 = 1.0 / jnp.full((1, TILE_LANES), corr1_ref[0], jnp.float32)
    scale2 = 1.0 / jnp.full((1, TILE_LANES), corr2_ref[0], jnp.float32)
    for rows, lanes, packed in tiles_of(numerator_ref.shape):
        new_moment1, new_moment2 = moments_of(landed_ref, moment1_ref, moment2_ref, rows, lanes)
        numerator = numerator_ref[rows, lanes]
        step = new_moment1 * scale1 / (jnp.sqrt(new_moment2 * scale2) + 1e-08)
        half = numerator - 0.05 * (step + 0.1 * numerator)
        half_ref[rows, lanes] = half
        payload_ref[packed, :] = half.astype(jnp.bfloat16)
    whole = jnp.full((TILE_ROWS, TILE_LANES), weight_ref[0], jnp.float32)
    high = whole.astype(jnp.bfloat16).astype(jnp.float32)
    middle = (whole - high).astype(jnp.bfloat16).astype(jnp.float32)
    low = whole - high - middle
    row = lax.broadcasted_iota(jnp.int32, whole.shape, 0)
    terms = jnp.where(row == 0, high, jnp.where(row == 1, middle, low))
    payload_ref[pl.ds(payload_ref.shape[0] - TILE_ROWS, TILE_ROWS), :] = terms.astype(jnp.bfloat16)


def received(rows, *refs):
    return sum(ref[rows, :].astype(jnp.float32) for ref in refs)


def weight_in(*refs):
    terms = received(pl.ds(refs[0].shape[0] - TILE_ROWS, TILE_ROWS), *refs)
    return terms[0:1] + (terms[1:2] + terms[2:3])


def mix_kernel(half_ref, own_ref, *refs):
    sent_refs, (new_numerator_ref, new_weight_ref, debiased_ref) = refs[:-3], refs[-3:]
    new_weight = 0.5 * (weight_in(own_ref) + weight_in(*sent_refs))
    new_weight_ref[0] = new_weight[0, 0]
    scale = 1.0 / new_weight
    for rows, lanes, packed in tiles_of(half_ref.shape):
        mixed = 0.5 * (half_ref[rows, lanes] + received(packed, *sent_refs))
        new_numerator_ref[rows, lanes] = mixed
        debiased_ref[rows, lanes] = (mixed * scale).astype(jnp.bfloat16)


def spec(space):
    return pl.BlockSpec(memory_space=space)


def call(kernel, out_shape, in_specs, out_specs, cost):
    return pl.pallas_call(
        kernel,
        out_shape=out_shape,
        in_specs=in_specs,
        out_specs=out_specs,
        compiler_params=pltpu.CompilerParams(vmem_limit_bytes=8 << 20),
        cost_estimate=pl.CostEstimate(flops=cost, bytes_accessed=cost, transcendentals=0),
        name=kernel.__name__,
    )


def exchanged(landed, moment1, moment2, half, payload, offset):
    shard = jax.ShapeDtypeStruct(half.shape, jnp.float32)
    scalars, arrays = spec(pltpu.SMEM), spec(pltpu.VMEM)
    sent = shifted(payload, "rep", offset)
    new_moment1, new_moment2 = call(
        moments_kernel, (shard, shard), [arrays] * 3, (arrays,) * 2, 4 * landed.size
    )(landed, moment1, moment2)
    new_numerator, new_weight, debiased = call(
        mix_kernel,
        (shard, jax.ShapeDtypeStruct((1,), jnp.float32), jax.ShapeDtypeStruct(half.shape, jnp.bfloat16)),
        [arrays] * (2 + len(sent)),
        (arrays, scalars, arrays),
        8 * half.size,
    )(half, payload, *sent)
    return (new_numerator[None], new_weight, debiased[None], new_moment1[None], new_moment2[None])


def local(step, numerator, weight, moment1, moment2, grads):
    levels = lax.axis_size("rep").bit_length() - 1
    n_fsdp = lax.axis_size("fsdp")
    rows, columns = numerator.shape[1:]
    count = (step + 1).astype(jnp.float32)
    first_corr = 1.0 - jnp.power(jnp.float32(0.9), count)
    second_corr = 1.0 - jnp.power(jnp.float32(0.95), count)
    blocks = grads.reshape(n_fsdp, rows, columns)
    landed = lax.all_to_all(blocks, "fsdp", split_axis=0, concat_axis=0, tiled=True)
    shard = jax.ShapeDtypeStruct((rows, columns), jnp.float32)
    packed_rows = rows * columns // TILE_LANES + TILE_ROWS
    scalars, arrays = spec(pltpu.SMEM), spec(pltpu.VMEM)
    half, payload = call(
        adam_kernel,
        (shard, jax.ShapeDtypeStruct((packed_rows, TILE_LANES), jnp.bfloat16)),
        [scalars] * 3 + [arrays] * 4,
        (arrays,) * 2,
        4 * landed.size,
    )(first_corr, second_corr, weight, landed, numerator[0], moment1[0], moment2[0])
    branches = [partial(exchanged, offset=1 << level) for level in range(levels)]
    return lax.switch(
        step[0] % levels, branches, landed, moment1[0], moment2[0], half, payload
    )


def solution(mesh):
    in_specs = (
        P(),
        P("rep", "fsdp", None),
        P("rep"),
        P("rep", "fsdp", None),
        P("rep", "fsdp", None),
        P("rep", "fsdp", None, None),
    )
    out_specs = (
        P("rep", "fsdp", None),
        P("rep"),
        P("rep", "fsdp", None),
        P("rep", "fsdp", None),
        P("rep", "fsdp", None),
    )
    return jax.shard_map(local, mesh=mesh, in_specs=in_specs, out_specs=out_specs, check_vma=False)
```

```python
from functools import partial

import jax
import jax.numpy as jnp
from jax import lax
from jax.experimental import pallas as pl
from jax.experimental.pallas import tpu as pltpu
from jax.sharding import PartitionSpec as P

TILE_ROWS = 16
TILE_LANES = 128


def shifted(value, axis, steps):
    count = lax.axis_size(axis)
    around = [(source, source + steps - count) for source in range(count - steps, count)]
    onward = [(source, source + steps) for source in range(count - steps)]
    first, second = around, onward
    if 2 * steps == count:
        first = [pair for pair in around + onward if pair[0] % 2 == 1]
        second = [pair for pair in around + onward if pair[0] % 2 == 0]
    return lax.ppermute(value, axis, second), lax.ppermute(value, axis, first)


def tiles_of(shape):
    across = shape[1] // TILE_LANES
    for down in range(shape[0] // TILE_ROWS):
        for column in range(across):
            rows = pl.ds(down * TILE_ROWS, TILE_ROWS)
            lanes = pl.ds(column * TILE_LANES, TILE_LANES)
            packed = pl.ds((down * across + column) * TILE_ROWS, TILE_ROWS)
            yield rows, lanes, packed


def moments_of(landed_ref, moment1_ref, moment2_ref, rows, lanes):
    sources = landed_ref.shape[0]
    total = landed_ref[0, rows, lanes].astype(jnp.float32)
    for source in range(1, sources):
        total = total + landed_ref[source, rows, lanes].astype(jnp.float32)
    new_moment1 = 0.9 * moment1_ref[rows, lanes] + (0.1 / sources) * total
    new_moment2 = 0.95 * moment2_ref[rows, lanes] + (0.05 / sources**2) * total * total
    return new_moment1, new_moment2


def moments_kernel(landed_ref, moment1_ref, moment2_ref, new_moment1_ref, new_moment2_ref):
    for rows, lanes, _ in tiles_of(moment1_ref.shape):
        new_moment1, new_moment2 = moments_of(landed_ref, moment1_ref, moment2_ref, rows, lanes)
        new_moment1_ref[rows, lanes] = new_moment1
        new_moment2_ref[rows, lanes] = new_moment2


def adam_kernel(
    corr1_ref, corr2_ref, weight_ref, landed_ref, numerator_ref, moment1_ref, moment2_ref,
    half_ref, payload_ref,
):
    scale1 = 0.05 / jnp.full((1, TILE_LANES), corr1_ref[0], jnp.float32)
    scale2 = 1.0 / jnp.full((1, TILE_LANES), corr2_ref[0], jnp.float32)
    for rows, lanes, packed in tiles_of(numerator_ref.shape):
        new_moment1, new_moment2 = moments_of(landed_ref, moment1_ref, moment2_ref, rows, lanes)
        second = new_moment2 * scale2
        root = second * lax.rsqrt(second)
        half = 0.995 * numerator_ref[rows, lanes] - new_moment1 * scale1 / (root + 1e-08)
        half_ref[rows, lanes] = half
        payload_ref[packed, :] = half.astype(jnp.bfloat16)
    whole = jnp.full((TILE_ROWS, TILE_LANES), weight_ref[0], jnp.float32)
    high = whole.astype(jnp.bfloat16).astype(jnp.float32)
    middle = (whole - high).astype(jnp.bfloat16).astype(jnp.float32)
    low = whole - high - middle
    row = lax.broadcasted_iota(jnp.int32, whole.shape, 0)
    terms = jnp.where(row == 0, high, jnp.where(row == 1, middle, low))
    payload_ref[pl.ds(payload_ref.shape[0] - TILE_ROWS, TILE_ROWS), :] = terms.astype(jnp.bfloat16)


def received(rows, *refs):
    return sum(ref[rows, :].astype(jnp.float32) for ref in refs)


def weight_in(*refs):
    terms = received(pl.ds(refs[0].shape[0] - TILE_ROWS, TILE_ROWS), *refs)
    return terms[0:1] + (terms[1:2] + terms[2:3])


def mix_kernel(half_ref, own_ref, *refs):
    sent_refs, (new_numerator_ref, new_weight_ref, debiased_ref) = refs[:-3], refs[-3:]
    new_weight = 0.5 * (weight_in(own_ref) + weight_in(*sent_refs))
    new_weight_ref[0] = new_weight[0, 0]
    scale = 1.0 / new_weight
    for rows, lanes, packed in tiles_of(half_ref.shape):
        mixed = 0.5 * (half_ref[rows, lanes] + received(packed, *sent_refs))
        new_numerator_ref[rows, lanes] = mixed
        debiased_ref[rows, lanes] = (mixed * scale).astype(jnp.bfloat16)


def spec(space):
    return pl.BlockSpec(memory_space=space)


def call(kernel, out_shape, in_specs, out_specs, cost):
    return pl.pallas_call(
        kernel,
        out_shape=out_shape,
        in_specs=in_specs,
        out_specs=out_specs,
        compiler_params=pltpu.CompilerParams(vmem_limit_bytes=8 << 20),
        cost_estimate=pl.CostEstimate(flops=cost, bytes_accessed=cost, transcendentals=0),
        name=kernel.__name__,
    )


def exchanged(landed, moment1, moment2, half, payload, offset):
    shard = jax.ShapeDtypeStruct(half.shape, jnp.float32)
    scalars, arrays = spec(pltpu.SMEM), spec(pltpu.VMEM)
    sent = shifted(payload, "rep", offset)
    new_moment1, new_moment2 = call(
        moments_kernel, (shard, shard), [arrays] * 3, (arrays,) * 2, 4 * landed.size
    )(landed, moment1, moment2)
    new_numerator, new_weight, debiased = call(
        mix_kernel,
        (shard, jax.ShapeDtypeStruct((1,), jnp.float32), jax.ShapeDtypeStruct(half.shape, jnp.bfloat16)),
        [arrays] * (2 + len(sent)),
        (arrays, scalars, arrays),
        8 * half.size,
    )(half, payload, *sent)
    return (new_numerator[None], new_weight, debiased[None], new_moment1[None], new_moment2[None])


def local(step, numerator, weight, moment1, moment2, grads):
    levels = lax.axis_size("rep").bit_length() - 1
    n_fsdp = lax.axis_size("fsdp")
    rows, columns = numerator.shape[1:]
    count = (step + 1).astype(jnp.float32)
    first_corr = 1.0 - jnp.power(jnp.float32(0.9), count)
    second_corr = 1.0 - jnp.power(jnp.float32(0.95), count)
    blocks = grads.reshape(n_fsdp, rows, columns)
    landed = lax.all_to_all(blocks, "fsdp", split_axis=0, concat_axis=0, tiled=True)
    shard = jax.ShapeDtypeStruct((rows, columns), jnp.float32)
    packed_rows = rows * columns // TILE_LANES + TILE_ROWS
    scalars, arrays = spec(pltpu.SMEM), spec(pltpu.VMEM)
    half, payload = call(
        adam_kernel,
        (shard, jax.ShapeDtypeStruct((packed_rows, TILE_LANES), jnp.bfloat16)),
        [scalars] * 3 + [arrays] * 4,
        (arrays,) * 2,
        4 * landed.size,
    )(first_corr, second_corr, weight, landed, numerator[0], moment1[0], moment2[0])
    branches = [partial(exchanged, offset=1 << level) for level in range(levels)]
    return lax.switch(
        step[0] % levels, branches, landed, moment1[0], moment2[0], half, payload
    )


def solution(mesh):
    in_specs = (
        P(),
        P("rep", "fsdp", None),
        P("rep"),
        P("rep", "fsdp", None),
        P("rep", "fsdp", None),
        P("rep", "fsdp", None, None),
    )
    out_specs = (
        P("rep", "fsdp", None),
        P("rep"),
        P("rep", "fsdp", None),
        P("rep", "fsdp", None),
        P("rep", "fsdp", None),
    )
    return jax.shard_map(local, mesh=mesh, in_specs=in_specs, out_specs=out_specs, check_vma=False)
```

```python
from functools import partial

import jax
import jax.numpy as jnp
from jax import lax
from jax.experimental import pallas as pl
from jax.experimental.pallas import tpu as pltpu
from jax.sharding import PartitionSpec as P

TILE_ROWS = 16
TILE_LANES = 128


def shifted(value, axis, steps):
    count = lax.axis_size(axis)
    around = [(source, source + steps - count) for source in range(count - steps, count)]
    onward = [(source, source + steps) for source in range(count - steps)]
    first, second = around, onward
    if 2 * steps == count:
        first = [pair for pair in around + onward if pair[0] % 2 == 1]
        second = [pair for pair in around + onward if pair[0] % 2 == 0]
    return lax.ppermute(value, axis, second), lax.ppermute(value, axis, first)


def tiles_of(shape):
    across = shape[1] // TILE_LANES
    for down in range(shape[0] // TILE_ROWS):
        for column in range(across):
            rows = pl.ds(down * TILE_ROWS, TILE_ROWS)
            lanes = pl.ds(column * TILE_LANES, TILE_LANES)
            packed = pl.ds((down * across + column) * TILE_ROWS, TILE_ROWS)
            yield rows, lanes, packed


def moments_of(landed_ref, moment1_ref, moment2_ref, rows, lanes):
    sources = landed_ref.shape[0]
    total = landed_ref[0, rows, lanes].astype(jnp.float32)
    for source in range(1, sources):
        total = total + landed_ref[source, rows, lanes].astype(jnp.float32)
    new_moment1 = 0.9 * moment1_ref[rows, lanes] + (0.1 / sources) * total
    new_moment2 = 0.95 * moment2_ref[rows, lanes] + (0.05 / sources**2) * total * total
    return new_moment1, new_moment2


def moments_kernel(landed_ref, moment1_ref, moment2_ref, new_moment1_ref, new_moment2_ref):
    for rows, lanes, _ in tiles_of(moment1_ref.shape):
        new_moment1, new_moment2 = moments_of(landed_ref, moment1_ref, moment2_ref, rows, lanes)
        new_moment1_ref[rows, lanes] = new_moment1
        new_moment2_ref[rows, lanes] = new_moment2


def adam_kernel(
    corr1_ref, corr2_ref, weight_ref, landed_ref, numerator_ref, moment1_ref, moment2_ref,
    half_ref, payload_ref,
):
    scale1 = 0.025 / jnp.full((1, TILE_LANES), corr1_ref[0], jnp.float32)
    scale2 = 1.0 / jnp.full((1, TILE_LANES), corr2_ref[0], jnp.float32)
    for rows, lanes, packed in tiles_of(numerator_ref.shape):
        new_moment1, new_moment2 = moments_of(landed_ref, moment1_ref, moment2_ref, rows, lanes)
        second = new_moment2 * scale2
        root = second * lax.rsqrt(second)
        half = 0.4975 * numerator_ref[rows, lanes] - new_moment1 * scale1 / (root + 1e-08)
        half_ref[rows, lanes] = half
        payload_ref[packed, :] = half.astype(jnp.bfloat16)
    whole = jnp.full((TILE_ROWS, TILE_LANES), weight_ref[0], jnp.float32)
    high = whole.astype(jnp.bfloat16).astype(jnp.float32)
    middle = (whole - high).astype(jnp.bfloat16).astype(jnp.float32)
    low = whole - high - middle
    row = lax.broadcasted_iota(jnp.int32, whole.shape, 0)
    terms = jnp.where(row == 0, high, jnp.where(row == 1, middle, low))
    payload_ref[pl.ds(payload_ref.shape[0] - TILE_ROWS, TILE_ROWS), :] = terms.astype(jnp.bfloat16)


def received(rows, *refs):
    return sum(ref[rows, :].astype(jnp.float32) for ref in refs)


def weight_in(*refs):
    terms = received(pl.ds(refs[0].shape[0] - TILE_ROWS, TILE_ROWS), *refs)
    return terms[0:1] + (terms[1:2] + terms[2:3])


def mix_kernel(half_ref, own_ref, *refs):
    sent_refs, (new_numerator_ref, new_weight_ref, debiased_ref) = refs[:-3], refs[-3:]
    new_weight = 0.5 * (weight_in(own_ref) + weight_in(*sent_refs))
    new_weight_ref[0] = new_weight[0, 0]
    scale = 1.0 / new_weight
    for rows, lanes, packed in tiles_of(half_ref.shape):
        mixed = half_ref[rows, lanes] + received(packed, *sent_refs)
        new_numerator_ref[rows, lanes] = mixed
        debiased_ref[rows, lanes] = (mixed * scale).astype(jnp.bfloat16)


def spec(space):
    return pl.BlockSpec(memory_space=space)


def call(kernel, out_shape, in_specs, out_specs, cost):
    return pl.pallas_call(
        kernel,
        out_shape=out_shape,
        in_specs=in_specs,
        out_specs=out_specs,
        compiler_params=pltpu.CompilerParams(vmem_limit_bytes=8 << 20),
        cost_estimate=pl.CostEstimate(flops=cost, bytes_accessed=cost, transcendentals=0),
        name=kernel.__name__,
    )


def exchanged(landed, moment1, moment2, half, payload, offset):
    shard = jax.ShapeDtypeStruct(half.shape, jnp.float32)
    scalars, arrays = spec(pltpu.SMEM), spec(pltpu.VMEM)
    sent = shifted(payload, "rep", offset)
    new_moment1, new_moment2 = call(
        moments_kernel, (shard, shard), [arrays] * 3, (arrays,) * 2, 4 * landed.size
    )(landed, moment1, moment2)
    new_numerator, new_weight, debiased = call(
        mix_kernel,
        (shard, jax.ShapeDtypeStruct((1,), jnp.float32), jax.ShapeDtypeStruct(half.shape, jnp.bfloat16)),
        [arrays] * (2 + len(sent)),
        (arrays, scalars, arrays),
        8 * half.size,
    )(half, payload, *sent)
    return (new_numerator[None], new_weight, debiased[None], new_moment1[None], new_moment2[None])


def local(step, numerator, weight, moment1, moment2, grads):
    levels = lax.axis_size("rep").bit_length() - 1
    n_fsdp = lax.axis_size("fsdp")
    rows, columns = numerator.shape[1:]
    count = (step + 1).astype(jnp.float32)
    first_corr = 1.0 - jnp.power(jnp.float32(0.9), count)
    second_corr = 1.0 - jnp.power(jnp.float32(0.95), count)
    blocks = grads.reshape(n_fsdp, rows, columns)
    landed = lax.all_to_all(blocks, "fsdp", split_axis=0, concat_axis=0, tiled=True)
    shard = jax.ShapeDtypeStruct((rows, columns), jnp.float32)
    packed_rows = rows * columns // TILE_LANES + TILE_ROWS
    scalars, arrays = spec(pltpu.SMEM), spec(pltpu.VMEM)
    half, payload = call(
        adam_kernel,
        (shard, jax.ShapeDtypeStruct((packed_rows, TILE_LANES), jnp.bfloat16)),
        [scalars] * 3 + [arrays] * 4,
        (arrays,) * 2,
        4 * landed.size,
    )(first_corr, second_corr, weight, landed, numerator[0], moment1[0], moment2[0])
    branches = [partial(exchanged, offset=1 << level) for level in range(levels)]
    return lax.switch(
        step[0] % levels, branches, landed, moment1[0], moment2[0], half, payload
    )


def solution(mesh):
    in_specs = (
        P(),
        P("rep", "fsdp", None),
        P("rep"),
        P("rep", "fsdp", None),
        P("rep", "fsdp", None),
        P("rep", "fsdp", None, None),
    )
    out_specs = (
        P("rep", "fsdp", None),
        P("rep"),
        P("rep", "fsdp", None),
        P("rep", "fsdp", None),
        P("rep", "fsdp", None),
    )
    return jax.shard_map(local, mesh=mesh, in_specs=in_specs, out_specs=out_specs, check_vma=False)
```

```python
from functools import partial

import jax
import jax.numpy as jnp
from jax import lax
from jax.experimental import pallas as pl
from jax.experimental.pallas import tpu as pltpu
from jax.sharding import PartitionSpec as P

TILE_ROWS = 16
TILE_LANES = 128


def shifted(value, axis, steps):
    count = lax.axis_size(axis)
    around = [(source, source + steps - count) for source in range(count - steps, count)]
    onward = [(source, source + steps) for source in range(count - steps)]
    first, second = around, onward
    if 2 * steps == count:
        first = [pair for pair in around + onward if pair[0] % 2 == 1]
        second = [pair for pair in around + onward if pair[0] % 2 == 0]
    return lax.ppermute(value, axis, second), lax.ppermute(value, axis, first)


def tiles_of(shape):
    across = shape[1] // TILE_LANES
    for down in range(shape[0] // TILE_ROWS):
        for column in range(across):
            rows = pl.ds(down * TILE_ROWS, TILE_ROWS)
            lanes = pl.ds(column * TILE_LANES, TILE_LANES)
            packed = pl.ds((down * across + column) * TILE_ROWS, TILE_ROWS)
            yield rows, lanes, packed


def moments_of(landed_ref, moment1_ref, moment2_ref, rows, lanes):
    sources = landed_ref.shape[0]
    terms = [landed_ref[source, rows, lanes].astype(jnp.float32) for source in range(sources)]
    while len(terms) > 1:
        terms = [sum(terms[at : at + 2]) for at in range(0, len(terms), 2)]
    total = terms[0]
    new_moment1 = 0.9 * moment1_ref[rows, lanes] + (0.1 / sources) * total
    new_moment2 = 0.95 * moment2_ref[rows, lanes] + (0.05 / sources**2) * total * total
    return new_moment1, new_moment2


def moments_kernel(landed_ref, moment1_ref, moment2_ref, new_moment1_ref, new_moment2_ref):
    for rows, lanes, _ in tiles_of(moment1_ref.shape):
        new_moment1, new_moment2 = moments_of(landed_ref, moment1_ref, moment2_ref, rows, lanes)
        new_moment1_ref[rows, lanes] = new_moment1
        new_moment2_ref[rows, lanes] = new_moment2


def adam_kernel(
    corr1_ref, corr2_ref, weight_ref, landed_ref, numerator_ref, moment1_ref, moment2_ref,
    half_ref, payload_ref,
):
    scale1 = 0.05 / jnp.full((1, TILE_LANES), corr1_ref[0], jnp.float32)
    scale2 = 1.0 / jnp.full((1, TILE_LANES), corr2_ref[0], jnp.float32)
    for rows, lanes, packed in tiles_of(numerator_ref.shape):
        new_moment1, new_moment2 = moments_of(landed_ref, moment1_ref, moment2_ref, rows, lanes)
        second = new_moment2 * scale2
        root = second * lax.rsqrt(second)
        half = 0.995 * numerator_ref[rows, lanes] - new_moment1 * scale1 / (root + 1e-08)
        half_ref[rows, lanes] = half
        payload_ref[packed, :] = half.astype(jnp.bfloat16)
    whole = jnp.full((TILE_ROWS, TILE_LANES), weight_ref[0], jnp.float32)
    high = whole.astype(jnp.bfloat16).astype(jnp.float32)
    middle = (whole - high).astype(jnp.bfloat16).astype(jnp.float32)
    low = whole - high - middle
    row = lax.broadcasted_iota(jnp.int32, whole.shape, 0)
    terms = jnp.where(row == 0, high, jnp.where(row == 1, middle, low))
    payload_ref[pl.ds(payload_ref.shape[0] - TILE_ROWS, TILE_ROWS), :] = terms.astype(jnp.bfloat16)


def received(rows, *refs):
    return sum(ref[rows, :].astype(jnp.float32) for ref in refs)


def weight_in(*refs):
    terms = received(pl.ds(refs[0].shape[0] - TILE_ROWS, TILE_ROWS), *refs)
    return terms[0:1] + (terms[1:2] + terms[2:3])


def mix_kernel(half_ref, own_ref, *refs):
    sent_refs, (new_numerator_ref, new_weight_ref, debiased_ref) = refs[:-3], refs[-3:]
    new_weight = 0.5 * (weight_in(own_ref) + weight_in(*sent_refs))
    new_weight_ref[0] = new_weight[0, 0]
    scale = 1.0 / new_weight
    for rows, lanes, packed in tiles_of(half_ref.shape):
        mixed = 0.5 * (half_ref[rows, lanes] + received(packed, *sent_refs))
        new_numerator_ref[rows, lanes] = mixed
        debiased_ref[rows, lanes] = (mixed * scale).astype(jnp.bfloat16)


def spec(space):
    return pl.BlockSpec(memory_space=space)


def call(kernel, out_shape, in_specs, out_specs, cost):
    return pl.pallas_call(
        kernel,
        out_shape=out_shape,
        in_specs=in_specs,
        out_specs=out_specs,
        compiler_params=pltpu.CompilerParams(vmem_limit_bytes=8 << 20),
        cost_estimate=pl.CostEstimate(flops=cost, bytes_accessed=cost, transcendentals=0),
        name=kernel.__name__,
    )


def exchanged(landed, moment1, moment2, half, payload, offset):
    shard = jax.ShapeDtypeStruct(half.shape, jnp.float32)
    scalars, arrays = spec(pltpu.SMEM), spec(pltpu.VMEM)
    sent = shifted(payload, "rep", offset)
    new_moment1, new_moment2 = call(
        moments_kernel, (shard, shard), [arrays] * 3, (arrays,) * 2, 4 * landed.size
    )(landed, moment1, moment2)
    new_numerator, new_weight, debiased = call(
        mix_kernel,
        (shard, jax.ShapeDtypeStruct((1,), jnp.float32), jax.ShapeDtypeStruct(half.shape, jnp.bfloat16)),
        [arrays] * (2 + len(sent)),
        (arrays, scalars, arrays),
        8 * half.size,
    )(half, payload, *sent)
    return (new_numerator[None], new_weight, debiased[None], new_moment1[None], new_moment2[None])


def local(step, numerator, weight, moment1, moment2, grads):
    levels = lax.axis_size("rep").bit_length() - 1
    n_fsdp = lax.axis_size("fsdp")
    rows, columns = numerator.shape[1:]
    count = (step + 1).astype(jnp.float32)
    first_corr = 1.0 - jnp.power(jnp.float32(0.9), count)
    second_corr = 1.0 - jnp.power(jnp.float32(0.95), count)
    blocks = grads.reshape(n_fsdp, rows, columns)
    landed = lax.all_to_all(blocks, "fsdp", split_axis=0, concat_axis=0, tiled=True)
    shard = jax.ShapeDtypeStruct((rows, columns), jnp.float32)
    packed_rows = rows * columns // TILE_LANES + TILE_ROWS
    scalars, arrays = spec(pltpu.SMEM), spec(pltpu.VMEM)
    half, payload = call(
        adam_kernel,
        (shard, jax.ShapeDtypeStruct((packed_rows, TILE_LANES), jnp.bfloat16)),
        [scalars] * 3 + [arrays] * 4,
        (arrays,) * 2,
        4 * landed.size,
    )(first_corr, second_corr, weight, landed, numerator[0], moment1[0], moment2[0])
    branches = [partial(exchanged, offset=1 << level) for level in range(levels)]
    return lax.switch(
        step[0] % levels, branches, landed, moment1[0], moment2[0], half, payload
    )


def solution(mesh):
    in_specs = (
        P(),
        P("rep", "fsdp", None),
        P("rep"),
        P("rep", "fsdp", None),
        P("rep", "fsdp", None),
        P("rep", "fsdp", None, None),
    )
    out_specs = (
        P("rep", "fsdp", None),
        P("rep"),
        P("rep", "fsdp", None),
        P("rep", "fsdp", None),
        P("rep", "fsdp", None),
    )
    return jax.shard_map(local, mesh=mesh, in_specs=in_specs, out_specs=out_specs, check_vma=False)
```
